512 devices in a mesh: ctx: 128 (over y, z, core), head: 4 (over x).
Axes of the slice: x: 4, y: 8, z: 8, core: 2. Of those that a mesh axis runs over, the one named last changes fastest.
Arguments:
- queries: bfloat16 [2, 16384, 8192], P(None, ('ctx', 'head')), may hold values from -25 to 25
- keys: bfloat16 [2, 16384, 1024], P(None, ('ctx', 'head')), may hold values from -5.5 to 5.5
- values: bfloat16 [2, 16384, 1024], P(None, ('ctx', 'head')), may hold values from -6 to 6
- doc_lengths: int32 [47], replicated, may hold values from 1 to 1408, 32768 in all
Outputs:
- attended: bfloat16 [2, 16384, 8192], P(None, ('ctx', 'head'))
The draws below stay inside these ranges and needn't reach their ends.
All inputs are finite; a program needn't handle non-finite values.
Results may differ from the reference program's by a relative error of at most 0.0045.
Values may be sent and summed in bfloat16 or wider, within the bound.
A program may use at most 64 MiB of HBM per device.

```python
import math
import jax
import jax.numpy as jnp
import numpy as np
from jax import lax

HD = 128
GROUP = 8
KVH = 8
BLOCK = 128
HQ = 64
RB = 11
HALF_LEN = 16384
DOC_MOST = 1408
DOCS = 47


def draw_queries(key, part):
    total_rows = 2 * HALF_LEN
    full = jnp.clip(jax.random.normal(jax.random.fold_in(key, 21), (total_rows, HQ * HD), jnp.float32), -5.5, 5.5)
    return full.reshape(2, HALF_LEN, HQ * HD).astype(jnp.bfloat16)


def draw_keys(key, part):
    total_rows = 2 * HALF_LEN
    full = jnp.clip(jax.random.normal(jax.random.fold_in(key, 31), (total_rows, KVH * HD), jnp.float32), -5.5, 5.5)
    return full.reshape(2, HALF_LEN, KVH * HD).astype(jnp.bfloat16)


def levels(stream_key, dims, split, low, top_value):
    def one(position, shards_of):
        steps = jax.random.uniform(jax.random.fold_in(jax.random.fold_in(stream_key, 6), position), (shards_of,), jnp.float32, low / len(split), top_value / len(split))
        return jnp.repeat(jnp.exp(steps), dims[position] // shards_of).reshape((-1,) + (1,) * (len(dims) - position - 1))

    loudness = one(*split[0])
    for cut in split[1:]:
        loudness = loudness * one(*cut)
    return loudness


def split_up(count, total, most, skew):
    portions = [(1 << 20) // math.isqrt(grade ** skew) + 1 for grade in range(2, count + 1)]
    rest, given = total - most - (count - 1), [1] * (count - 1)
    while rest > 0:
        candidates = [i for i in range(count - 1) if given[i] < most]
        whole, budget = sum([portions[i] for i in candidates]), rest
        for i in candidates:
            more = min(most - given[i], max(1, budget * portions[i] // whole), rest)
            given[i] = given[i] + more
            rest = rest - more
    return np.array([most] + given)


def ragged(rng, amount, total, limit, skew):
    if amount == 2:
        one = jax.random.randint(rng, (), max(1, total - limit), min(limit, total - 1) + 1)
        return jnp.stack([one, total - one])
    tallies = jnp.asarray(split_up(amount, total, limit, skew), jnp.int32)
    pairs = (amount - 1) // 2
    source_of, receiver = tallies[1:1 + 2 * pairs:2], tallies[2:2 + 2 * pairs:2]
    margin = jnp.minimum(source_of - 1, limit - receiver)
    shifted = jax.random.randint(jax.random.fold_in(rng, 1), (pairs,), 0, 1 << 20) % (margin + 1)
    tallies = tallies.at[1:1 + 2 * pairs:2].set(source_of - shifted).at[2:2 + 2 * pairs:2].set(receiver + shifted)
    return tallies[jax.random.permutation(jax.random.fold_in(rng, 2), amount)]


def scatter_about(own_key, dims, deviation, most, split=(), kind=jnp.bfloat16):
    loudness = levels(own_key, dims, split, -0.22, 0.18) if split else 1.0
    values = jax.random.normal(own_key, dims, jnp.float32) * deviation * loudness
    return jnp.minimum(jnp.maximum(values, -most), most).astype(kind)


def setup_inputs(seed: int = 0) -> dict:
    key_of = jax.random.split(jax.random.key(seed), 5)
    queries = draw_queries(jax.random.fold_in(key_of[4], 71), 0)
    keys = draw_keys(jax.random.fold_in(key_of[4], 71), 0)
    values = scatter_about(key_of[2], (2, HALF_LEN, KVH * HD), 1.0, 6.0, ((1, 512),))
    doc_lengths = ragged(key_of[3], DOCS, 2 * HALF_LEN, DOC_MOST, 2).astype(jnp.int32)
    return {"queries": queries, "keys": keys, "values": values, "doc_lengths": doc_lengths}


NEG_FILL = -1e+30

def doc_of(positions, ends):
    return lax.optimization_barrier(jnp.sum((positions[:, None] >= ends[None, :]).astype(jnp.int32), axis=1))

def reference(queries, keys, values, doc_lengths):
    length = 2 * HALF_LEN
    span = RB * BLOCK
    query_rows = queries.reshape(length, KVH, GROUP, HD)
    key_rows = keys.reshape(length, KVH, HD)
    value_rows = values.reshape(length, KVH, HD)
    pad_keys = jnp.concatenate([jnp.zeros((span, KVH, HD), key_rows.dtype), key_rows], axis=0)
    pad_values = jnp.concatenate([jnp.zeros((span, KVH, HD), value_rows.dtype), value_rows], axis=0)
    ends = jnp.cumsum(doc_lengths).astype(jnp.int32)
    scale = 1.0 / math.sqrt(HD)

    def one_block(index):
        start = (index * BLOCK).astype(jnp.int32)
        q_block = lax.dynamic_slice_in_dim(query_rows, start, BLOCK, 0).astype(jnp.float32)
        k_block = lax.dynamic_slice_in_dim(pad_keys, start, span + BLOCK, 0).astype(jnp.float32)
        v_block = lax.dynamic_slice_in_dim(pad_values, start, span + BLOCK, 0).astype(jnp.float32)
        query_pos = start + jnp.arange(BLOCK, dtype=jnp.int32)
        key_pos = start - span + jnp.arange(span + BLOCK, dtype=jnp.int32)
        allowed = (doc_of(query_pos, ends)[:, None] == doc_of(key_pos, ends)[None, :]) & (key_pos[None, :] <= query_pos[:, None]) & (key_pos[None, :] >= 0)
        scores = jnp.einsum('rkgd,skd->kgrs', q_block, k_block) * scale
        masked = jnp.where(allowed[None, None], scores, NEG_FILL)
        top = lax.optimization_barrier(jnp.max(masked, axis=3, keepdims=True))
        weights = jnp.where(allowed[None, None], jnp.exp(masked - top), 0.0)
        total = lax.optimization_barrier(jnp.sum(weights, axis=3))
        rounded = lax.optimization_barrier(weights.astype(jnp.bfloat16))
        mixed = jnp.einsum('kgrs,skd->rkgd', rounded.astype(jnp.float32), v_block)
        mixed = mixed / jnp.transpose(total, (2, 0, 1))[..., None]
        return mixed.reshape(BLOCK, HQ * HD).astype(jnp.bfloat16)
    blocks = lax.map(one_block, jnp.arange(length // BLOCK, dtype=jnp.int32))
    return blocks.reshape(2, HALF_LEN, HQ * HD)
```

```python
import functools
import math

import jax
import jax.numpy as jnp
from jax import lax
from jax.experimental import pallas as pl
from jax.experimental.pallas import tpu as pltpu
from jax.sharding import PartitionSpec as P

MESH = pl.DeviceIdType.MESH
HD = 128
HEADS = 8
GROUP = 8
SIDE = 4
GROUP_SIZE = 8
SLOTS = 7
NEG_FILL = -1e30
FACTOR = 1.0 / math.sqrt(HD) * math.log2(math.e)


def attention_kernel(
    rows,
    groups,
    half_len,
    q_ref,
    k_ref,
    v_ref,
    len_ref,
    out_ref,
    q_all,
    k_win,
    v_win,
    o_all,
    bias,
    scores,
    sent,
    own_sem,
    q_sem,
    up_sem,
    down_sem,
    chain_sent,
    out_sem,
):
    ctx = lax.axis_index("ctx")
    x = lax.axis_index("head")
    core = lax.rem(ctx, 2)
    group = ctx // 2
    me = core * SIDE + x
    span = rows * GROUP_SIZE
    block = span // 2
    wide = GROUP * HD
    own_row = (SLOTS - 1) * span
    window = (SLOTS - 2) * span + 2 * block

    def member(index):
        return (group * 2 + index // SIDE, lax.rem(index, SIDE))

    def along(step):
        return (lax.rem(group + step + groups, groups) * 2 + core, x)

    barrier = pltpu.get_barrier_semaphore()
    for k in range(1, GROUP_SIZE):
        other = member(lax.rem(me + k, GROUP_SIZE))
        pl.semaphore_signal(barrier, inc=1, device_id=other, device_id_type=MESH)
    for step in (1, -1, SLOTS - 1, 1 - SLOTS):
        pl.semaphore_signal(barrier, inc=1, device_id=along(step), device_id_type=MESH)
    pl.semaphore_wait(barrier, GROUP_SIZE + 3)

    my_rows = pl.ds(pl.multiple_of(own_row + me * rows, rows), rows)
    for which, (src, dst) in enumerate(((k_ref, k_win), (v_ref, v_win))):
        for half in range(2):
            for k in range(GROUP_SIZE):
                index = lax.rem(me + k, GROUP_SIZE)
                cols = pl.ds(pl.multiple_of(index * HD, HD), HD)
                if k:
                    pltpu.make_async_remote_copy(
                        src.at[half, :, cols],
                        dst.at[half, my_rows, :],
                        sent.at[which],
                        own_sem.at[which, half],
                        device_id=member(index),
                        device_id_type=MESH,
                    ).start()
                else:
                    pltpu.make_async_copy(
                        src.at[half, :, cols], dst.at[half, my_rows, :], own_sem.at[which, half]
                    ).start()

    q_rows = pl.ds(pl.multiple_of(me * rows, rows), rows)
    for half in range(2):
        for k in range(GROUP_SIZE):
            index = lax.rem(me + k, GROUP_SIZE)
            cols = pl.ds(pl.multiple_of(index * wide, wide), wide)
            if k:
                pltpu.make_async_remote_copy(
                    q_ref.at[half, :, cols],
                    q_all.at[half, q_rows, :],
                    sent.at[2],
                    q_sem.at[half],
                    device_id=member(index),
                    device_id_type=MESH,
                ).start()
            else:
                pltpu.make_async_copy(q_ref.at[half, :, cols], q_all.at[half, q_rows, :], q_sem.at[half]).start()

    def slot_rows(slot):
        return pl.ds((SLOTS - 1 - slot) * span, span)

    def hop(which, half, from_slot, to_slot, step, sem):
        ref = (k_win, v_win)[which]
        crossed = (group + step + groups) // groups - 1
        to_half = lax.rem(half + crossed + 2, 2)
        return pltpu.make_async_remote_copy(
            ref.at[half, slot_rows(from_slot), :],
            ref.at[to_half, slot_rows(to_slot), :],
            chain_sent.at[which],
            sem.at[to_half],
            device_id=along(step),
            device_id_type=MESH,
        )

    def arrived(which, half, slot, sem):
        ref = (k_win, v_win)[which].at[half, slot_rows(slot), :]
        pltpu.make_async_copy(ref, ref, sem.at[half]).wait()

    for which in range(2):
        for half in range(2):
            arrived(which, half, 0, own_sem.at[which])
            hop(which, half, 0, 1, 1, up_sem.at[0, which]).start()
            hop(which, half, 0, 6, 6, down_sem.at[0, which]).start()

    for half in range(2):
        for part in range(2):
            first = half * half_len + group * span + part * block
            pos = first + lax.broadcasted_iota(jnp.int32, (block, 1), 0)

            def one_doc(i, carry):
                end, begin = carry
                end = end + len_ref[i]
                return end, jnp.where(pos >= end, end, begin)

            _, begin = lax.fori_loop(0, len_ref.shape[0], one_doc, (jnp.int32(0), jnp.zeros((block, 1), jnp.int32)))
            key_pos = first - (window - block) + lax.broadcasted_iota(jnp.int32, (1, window), 1)
            allowed = (key_pos >= begin) & (key_pos <= pos)
            bias[half * 2 + part] = jnp.where(allowed, 0.0, NEG_FILL)

    for step in range(3):
        for which in range(2):
            for half in range(2):
                arrived(which, half, step + 1, up_sem.at[step, which])
                if step < 2 or which == 0:
                    hop(which, half, step + 1, step + 2, 1, up_sem.at[step + 1, which]).start()
                if step < 2:
                    arrived(which, half, 6 - step, down_sem.at[step, which])
                    if step == 0 or which == 1:
                        hop(which, half, 6 - step, 5 - step, -1, down_sem.at[step + 1, which]).start()

    def unit(u, half):
        part = u // 2
        side = lax.rem(u, 2)
        row0 = pl.multiple_of(part * block, block)
        col0 = pl.multiple_of(side * (wide // 2), wide // 2)
        keys_from = pl.multiple_of(block + part * block, block)
        queries = jnp.concatenate(
            [
                q_all[half, pl.ds(row0, block), pl.ds(pl.multiple_of(col0 + i * HD, HD), HD)]
                for i in range(GROUP // 2)
            ],
            axis=0,
        )
        keys = k_win[half, pl.ds(keys_from, window), :]
        for tile in range(window // 256):
            part_keys = keys[tile * 256 : (tile + 1) * 256]
            product = lax.dot_general(
                queries, part_keys, (((1,), (1,)), ((), ())), preferred_element_type=jnp.float32
            )
            add = bias[half * 2 + part, :, tile * 256 : (tile + 1) * 256]
            scores[:, tile * 256 : (tile + 1) * 256] = (
                product.reshape(GROUP // 2, block, 256) + add[None]
            ).reshape(GROUP // 2 * block, 256)
        values = v_win[half, pl.ds(keys_from, window), :]
        values = jnp.concatenate([values, jnp.ones_like(values)], axis=1)
        for i in range(GROUP // 2):
            s = scores[i * block : (i + 1) * block, :]
            top = jnp.max(s, axis=1, keepdims=True)
            weight = jnp.exp2((s - top) * FACTOR).astype(jnp.bfloat16)
            mixed = jnp.dot(weight, values, preferred_element_type=jnp.float32)
            o_all[half * 4 + u, :, i * HD : (i + 1) * HD] = (mixed[:, :HD] / mixed[:, HD:]).astype(jnp.bfloat16)
        for k in range(SIDE):
            to_x = lax.rem(x + k, SIDE)
            src = o_all.at[half * 4 + u, pl.ds(pl.multiple_of(to_x * rows, rows), rows), :]
            dst = out_ref.at[half, :, pl.ds(pl.multiple_of(me * wide + col0, wide // 2), wide // 2)]

            def remote():
                pltpu.make_async_remote_copy(
                    src,
                    dst,
                    sent.at[3],
                    out_sem,
                    device_id=(group * 2 + part, to_x),
                    device_id_type=MESH,
                ).start()

            if k:
                remote()
            else:
                pl.when(part != core)(remote)

                @pl.when(part == core)
                def _():
                    pltpu.make_async_copy(src, dst, out_sem).start()

        return 0

    for half in range(2):
        pltpu.make_async_copy(q_all.at[half], q_all.at[half], q_sem.at[half]).wait()
        arrived(0, half, 4, up_sem.at[3, 0])
        arrived(1, half, 4, down_sem.at[2, 1])
    for half in range(2):
        lax.fori_loop(0, 4, lambda u, _, half=half: unit(u, half), 0)

    pltpu.make_async_copy(out_ref, out_ref, out_sem).wait()
    others = k_ref.at[:, :, : (GROUP_SIZE - 1) * HD]
    pltpu.make_async_copy(others, others, sent.at[0]).wait()
    pltpu.make_async_copy(others, others, sent.at[1]).wait()
    others = q_ref.at[:, :, : (GROUP_SIZE - 1) * wide]
    pltpu.make_async_copy(others, others, sent.at[2]).wait()
    pltpu.make_async_copy(others, others, sent.at[3]).wait()
    for which in range(2):
        hops = (k_win, v_win)[which].at[:, pl.ds(0, 6 * span), :]
        pltpu.make_async_copy(hops, hops, chain_sent.at[which]).wait()


def per_device(queries, keys, values, doc_lengths):
    rows = queries.shape[1]
    groups = lax.axis_size("ctx") // 2
    half_len = rows * GROUP_SIZE * groups
    span = rows * GROUP_SIZE
    block = span // 2
    window = (SLOTS - 1) * span
    pairs = 2 * span * GROUP
    body = functools.partial(attention_kernel, rows, groups, half_len)
    anywhere = pl.BlockSpec(memory_space=pl.ANY)
    return pl.pallas_call(
        body,
        out_shape=jax.ShapeDtypeStruct(queries.shape, queries.dtype),
        in_specs=[anywhere, anywhere, anywhere, pl.BlockSpec(memory_space=pltpu.SMEM)],
        out_specs=anywhere,
        scratch_shapes=[
            pltpu.VMEM((2, span, GROUP * HD), jnp.bfloat16),
            pltpu.VMEM((2, SLOTS * span, HD), jnp.bfloat16),
            pltpu.VMEM((2, SLOTS * span, HD), jnp.bfloat16),
            pltpu.VMEM((8, block, GROUP // 2 * HD), jnp.bfloat16),
            pltpu.VMEM((4, block, window), jnp.float32),
            pltpu.VMEM((GROUP // 2 * block, window), jnp.float32),
            pltpu.SemaphoreType.DMA((4,)),
            pltpu.SemaphoreType.DMA((2, 2)),
            pltpu.SemaphoreType.DMA((2,)),
            pltpu.SemaphoreType.DMA((4, 2, 2)),
            pltpu.SemaphoreType.DMA((3, 2, 2)),
            pltpu.SemaphoreType.DMA((2,)),
            pltpu.SemaphoreType.DMA,
        ],
        compiler_params=pltpu.CompilerParams(
            collective_id=0, has_side_effects=True, vmem_limit_bytes=48 << 20
        ),
        cost_estimate=pl.CostEstimate(
            flops=4 * pairs * window * HD, bytes_accessed=5 << 20, transcendentals=pairs * window
        ),
    )(queries, keys, values, doc_lengths)


def solution(mesh):
    placed = P(None, ("ctx", "head"), None)
    return jax.shard_map(
        per_device,
        mesh=mesh,
        in_specs=(placed, placed, placed, P()),
        out_specs=placed,
        check_vma=False,
    )
```

```python
import functools
import math

import jax
import jax.numpy as jnp
from jax import lax
from jax.experimental import pallas as pl
from jax.experimental.pallas import tpu as pltpu
from jax.sharding import PartitionSpec as P

MESH = pl.DeviceIdType.MESH
HD = 128
HEADS = 8
GROUP = 8
SIDE = 4
GROUP_SIZE = 8
SLOTS = 7
NEG_FILL = -1e30
ORDER = (
    ("up", 0, 0, 0), ("down", 0, 0, 0), ("up", 0, 0, 1), ("down", 0, 0, 1),
    ("up", 0, 1, 0), ("down", 0, 1, 0), ("up", 0, 1, 1), ("down", 0, 1, 1),
    ("up", 1, 0, 0), ("up", 1, 0, 1), ("up", 1, 1, 0), ("up", 1, 1, 1),
    ("up", 2, 0, 0), ("up", 2, 0, 1), ("up", 2, 1, 0), ("up", 2, 1, 1),
    ("down", 6, 0, 0), ("down", 6, 0, 1), ("down", 6, 1, 0), ("down", 6, 1, 1),
    ("up", 3, 0, 0), ("up", 3, 0, 1), ("up", 3, 1, 0), ("up", 3, 1, 1),
    ("down", 5, 0, 0), ("down", 5, 0, 1), ("down", 5, 1, 0), ("down", 5, 1, 1),
    ("up", 4, 0, 0), ("down", 4, 0, 1), (), ("up", 4, 1, 0), ("down", 4, 1, 1),
)
FACTOR = 1.0 / math.sqrt(HD) * math.log2(math.e)


def attention_kernel(
    rows,
    groups,
    half_len,
    q_ref,
    k_ref,
    v_ref,
    len_ref,
    out_ref,
    q_all,
    k_low,
    k_high,
    v_low,
    v_high,
    o_all,
    bias,
    scores,
    sent,
    own_sem,
    q_sem,
    up_sem,
    down_sem,
    chain_sent,
    out_sem,
):
    ctx = lax.axis_index("ctx")
    x = lax.axis_index("head")
    core = lax.rem(ctx, 2)
    group = ctx // 2
    me = core * SIDE + x
    span = rows * GROUP_SIZE
    block = span // 2
    wide = GROUP * HD
    own_row = (SLOTS - 1) * span
    window = (SLOTS - 2) * span + 2 * block

    windows = ((k_low, k_high), (v_low, v_high))

    def member(index):
        return (group * 2 + index // SIDE, lax.rem(index, SIDE))

    def along(step):
        return (lax.rem(group + step + groups, groups) * 2 + core, x)

    barrier = pltpu.get_barrier_semaphore()
    for k in range(1, GROUP_SIZE):
        other = member(lax.rem(me + k, GROUP_SIZE))
        pl.semaphore_signal(barrier, inc=1, device_id=other, device_id_type=MESH)
    for step in (1, -1, SLOTS - 1, 1 - SLOTS):
        pl.semaphore_signal(barrier, inc=1, device_id=along(step), device_id_type=MESH)
    pl.semaphore_wait(barrier, GROUP_SIZE + 3)

    my_rows = pl.ds(pl.multiple_of(own_row + me * rows, rows), rows)
    for half in range(2):
        for which, src in enumerate((k_ref, v_ref)):
            dst = windows[which][half]
            for k in range(GROUP_SIZE):
                index = lax.rem(me + k, GROUP_SIZE)
                cols = pl.ds(pl.multiple_of(index * HD, HD), HD)
                if k:
                    pltpu.make_async_remote_copy(
                        src.at[half, :, cols],
                        dst.at[my_rows, :],
                        sent.at[which],
                        own_sem.at[which, half],
                        device_id=member(index),
                        device_id_type=MESH,
                    ).start()
                else:
                    pltpu.make_async_copy(
                        src.at[half, :, cols], dst.at[my_rows, :], own_sem.at[which, half]
                    ).start()

    q_rows = pl.ds(pl.multiple_of(me * rows, rows), rows)
    for half in range(2):
        for k in range(GROUP_SIZE):
            index = lax.rem(me + k, GROUP_SIZE)
            cols = pl.ds(pl.multiple_of(index * wide, wide), wide)
            if k:
                pltpu.make_async_remote_copy(
                    q_ref.at[half, :, cols],
                    q_all.at[half, q_rows, :],
                    sent.at[2],
                    q_sem.at[half],
                    device_id=member(index),
                    device_id_type=MESH,
                ).start()
            else:
                pltpu.make_async_copy(q_ref.at[half, :, cols], q_all.at[half, q_rows, :], q_sem.at[half]).start()

    def slot_rows(slot):
        return pl.ds((SLOTS - 1 - slot) * span, span)

    def hop(which, half, from_slot, to_slot, step, sem):
        crossed = (group + step + groups) // groups - 1

        def to(to_half):
            pltpu.make_async_remote_copy(
                windows[which][half].at[slot_rows(from_slot), :],
                windows[which][to_half].at[slot_rows(to_slot), :],
                chain_sent.at[which, half],
                sem.at[to_half],
                device_id=along(step),
                device_id_type=MESH,
            ).start()

        pl.when(crossed == 0)(lambda: to(half))
        pl.when(crossed != 0)(lambda: to(1 - half))

    def arrived(which, half, slot, sem):
        ref = windows[which][half].at[slot_rows(slot), :]
        pltpu.make_async_copy(ref, ref, sem.at[half]).wait()

    for half in range(2):
        for part in range(2):
            first = half * half_len + group * span + part * block
            pos = first + lax.broadcasted_iota(jnp.int32, (block, 1), 0)

            def one_doc(i, carry):
                end, begin = carry
                end = end + len_ref[i]
                return end, jnp.where(pos >= end, end, begin)

            _, begin = lax.fori_loop(0, len_ref.shape[0], one_doc, (jnp.int32(0), jnp.zeros((block, 1), jnp.int32)))
            key_pos = first - (window - block) + lax.broadcasted_iota(jnp.int32, (1, window), 1)
            allowed = (key_pos >= begin) & (key_pos <= pos)
            bias[half * 2 + part] = jnp.where(allowed, 0.0, NEG_FILL)

    awaited = set()

    def pass_on(way, slot, half, which):
        if slot == 0 and (half, which) not in awaited:
            awaited.add((half, which))
            arrived(which, half, 0, own_sem.at[which])
        if way == "up":
            if slot > 0:
                arrived(which, half, slot, up_sem.at[slot - 1, which])
            if slot < 3 or (slot == 3 and which == 0):
                hop(which, half, slot, slot + 1, 1, up_sem.at[slot, which])
        elif slot == 0:
            hop(which, half, 0, 6, 6, down_sem.at[0, which])
        else:
            arrived(which, half, slot, down_sem.at[6 - slot, which])
            if slot == 6 or (slot == 5 and which == 1):
                hop(which, half, slot, slot - 1, -1, down_sem.at[7 - slot, which])

    def unit(u, half):
        part = u // 2
        side = lax.rem(u, 2)
        row0 = pl.multiple_of(part * block, block)
        col0 = pl.multiple_of(side * (wide // 2), wide // 2)
        keys_from = pl.multiple_of(block + part * block, block)
        queries = jnp.concatenate(
            [
                q_all[half, pl.ds(row0, block), pl.ds(pl.multiple_of(col0 + i * HD, HD), HD)]
                for i in range(GROUP // 2)
            ],
            axis=0,
        )
        keys = windows[0][half][pl.ds(keys_from, window), :]
        for tile in range(window // 256):
            part_keys = keys[tile * 256 : (tile + 1) * 256]
            product = lax.dot_general(
                queries, part_keys, (((1,), (1,)), ((), ())), preferred_element_type=jnp.float32
            )
            add = bias[half * 2 + part, :, tile * 256 : (tile + 1) * 256]
            scores[:, tile * 256 : (tile + 1) * 256] = (
                product.reshape(GROUP // 2, block, 256) + add[None]
            ).reshape(GROUP // 2 * block, 256)
        values = windows[1][half][pl.ds(keys_from, window), :]
        values = jnp.concatenate([values, jnp.ones_like(values)], axis=1)
        for i in range(GROUP // 2):
            s = scores[i * block : (i + 1) * block, :]
            top = jnp.max(s, axis=1, keepdims=True)
            weight = jnp.exp2((s - top) * FACTOR).astype(jnp.bfloat16)
            mixed = jnp.dot(weight, values, preferred_element_type=jnp.float32)
            o_all[half * 4 + u, :, i * HD : (i + 1) * HD] = (mixed[:, :HD] / mixed[:, HD:]).astype(jnp.bfloat16)
        for k in range(SIDE):
            to_x = lax.rem(x + k, SIDE)
            src = o_all.at[half * 4 + u, pl.ds(pl.multiple_of(to_x * rows, rows), rows), :]
            dst = out_ref.at[half, :, pl.ds(pl.multiple_of(me * wide + col0, wide // 2), wide // 2)]

            def remote():
                pltpu.make_async_remote_copy(
                    src,
                    dst,
                    sent.at[3],
                    out_sem,
                    device_id=(group * 2 + part, to_x),
                    device_id_type=MESH,
                ).start()

            if k:
                remote()
            else:
                pl.when(part != core)(remote)

                @pl.when(part == core)
                def _():
                    pltpu.make_async_copy(src, dst, out_sem).start()

        return 0

    for entry in ORDER:
        if entry:
            pass_on(*entry)
        else:
            for half in range(2):
                pltpu.make_async_copy(q_all.at[half], q_all.at[half], q_sem.at[half]).wait()
            lax.fori_loop(0, 4, lambda u, _: unit(u, 0), 0)
    lax.fori_loop(0, 4, lambda u, _: unit(u, 1), 0)

    pltpu.make_async_copy(out_ref, out_ref, out_sem).wait()
    others = k_ref.at[:, :, : (GROUP_SIZE - 1) * HD]
    pltpu.make_async_copy(others, others, sent.at[0]).wait()
    pltpu.make_async_copy(others, others, sent.at[1]).wait()
    others = q_ref.at[:, :, : (GROUP_SIZE - 1) * wide]
    pltpu.make_async_copy(others, others, sent.at[2]).wait()
    pltpu.make_async_copy(others, others, sent.at[3]).wait()
    for which in range(2):
        for half in range(2):
            hops = windows[which][half].at[pl.ds(0, 6 * span), :]
            pltpu.make_async_copy(hops, hops, chain_sent.at[which, half]).wait()


def per_device(queries, keys, values, doc_lengths):
    rows = queries.shape[1]
    groups = lax.axis_size("ctx") // 2
    half_len = rows * GROUP_SIZE * groups
    span = rows * GROUP_SIZE
    block = span // 2
    window = (SLOTS - 1) * span
    pairs = 2 * span * GROUP
    body = functools.partial(attention_kernel, rows, groups, half_len)
    anywhere = pl.BlockSpec(memory_space=pl.ANY)
    return pl.pallas_call(
        body,
        out_shape=jax.ShapeDtypeStruct(queries.shape, queries.dtype),
        in_specs=[anywhere, anywhere, anywhere, pl.BlockSpec(memory_space=pltpu.SMEM)],
        out_specs=anywhere,
        scratch_shapes=[
            pltpu.VMEM((2, span, GROUP * HD), jnp.bfloat16),
            pltpu.VMEM((SLOTS * span, HD), jnp.bfloat16),
            pltpu.VMEM((SLOTS * span, HD), jnp.bfloat16),
            pltpu.VMEM((SLOTS * span, HD), jnp.bfloat16),
            pltpu.VMEM((SLOTS * span, HD), jnp.bfloat16),
            pltpu.VMEM((8, block, GROUP // 2 * HD), jnp.bfloat16),
            pltpu.VMEM((4, block, window), jnp.float32),
            pltpu.VMEM((GROUP // 2 * block, window), jnp.float32),
            pltpu.SemaphoreType.DMA((4,)),
            pltpu.SemaphoreType.DMA((2, 2)),
            pltpu.SemaphoreType.DMA((2,)),
            pltpu.SemaphoreType.DMA((4, 2, 2)),
            pltpu.SemaphoreType.DMA((3, 2, 2)),
            pltpu.SemaphoreType.DMA((2, 2)),
            pltpu.SemaphoreType.DMA,
        ],
        compiler_params=pltpu.CompilerParams(
            collective_id=0, has_side_effects=True, vmem_limit_bytes=63 << 20
        ),
        cost_estimate=pl.CostEstimate(
            flops=4 * pairs * window * HD, bytes_accessed=5 << 20, transcendentals=pairs * window
        ),
    )(queries, keys, values, doc_lengths)


def solution(mesh):
    placed = P(None, ("ctx", "head"), None)
    return jax.shard_map(
        per_device,
        mesh=mesh,
        in_specs=(placed, placed, placed, P()),
        out_specs=placed,
        check_vma=False,
    )
```

```python
import functools
import math

import jax
import jax.numpy as jnp
from jax import lax
from jax.experimental import pallas as pl
from jax.experimental.pallas import tpu as pltpu
from jax.sharding import PartitionSpec as P

MESH = pl.DeviceIdType.MESH
HD = 128
HEADS = 8
GROUP = 8
SIDE = 4
GROUP_SIZE = 8
SLOTS = 7
RING = 8
NEG_FILL = -1e30
ORDER = (
    ("up", 0, 0, 0), ("down", 0, 0, 0), ("up", 0, 0, 1), ("down", 0, 0, 1),
    ("up", 0, 1, 0), ("down", 0, 1, 0), ("up", 0, 1, 1), ("down", 0, 1, 1),
    ("up", 1, 0, 0), ("up", 1, 0, 1), ("up", 1, 1, 0), ("up", 1, 1, 1),
    ("relay", 0, 0, 0), ("relay", 0, 0, 1), ("relay", 0, 1, 0), ("relay", 0, 1, 1),
    ("up", 2, 0, 0), ("up", 2, 0, 1), ("up", 2, 1, 0), ("up", 2, 1, 1),
    ("down", 6, 0, 0), ("down", 6, 0, 1), ("down", 6, 1, 0), ("down", 6, 1, 1),
    ("up", 3, 0, 0), ("up", 3, 0, 1), ("up", 3, 1, 0), ("up", 3, 1, 1),
    ("down", 5, 0, 0), ("down", 5, 0, 1), ("down", 5, 1, 0), ("down", 5, 1, 1),
    ("up", 4, 0, 0), ("down", 4, 0, 1), (), ("up", 4, 1, 0), ("down", 4, 1, 1),
)
FACTOR = 1.0 / math.sqrt(HD) * math.log2(math.e)


def attention_kernel(
    rows,
    groups,
    half_len,
    q_ref,
    k_ref,
    v_ref,
    len_ref,
    out_ref,
    q_all,
    k_low,
    k_high,
    v_low,
    v_high,
    relayed,
    o_all,
    bias,
    scores,
    sent,
    own_sem,
    q_sem,
    up_sem,
    down_sem,
    chain_sent,
    relay_sem,
    relay_sent,
    out_sem,
):
    ctx = lax.axis_index("ctx")
    x = lax.axis_index("head")
    core = lax.rem(ctx, 2)
    group = ctx // 2
    place = lax.rem(group, RING)
    me = core * SIDE + x
    span = rows * GROUP_SIZE
    block = span // 2
    wide = GROUP * HD
    own_row = (SLOTS - 1) * span
    window = (SLOTS - 2) * span + 2 * block

    windows = ((k_low, k_high), (v_low, v_high))

    def member(index):
        return (group * 2 + index // SIDE, lax.rem(index, SIDE))

    def along(step):
        return (lax.rem(group + step + groups, groups) * 2 + core, x)

    barrier = pltpu.get_barrier_semaphore()
    for k in range(1, GROUP_SIZE):
        other = member(lax.rem(me + k, GROUP_SIZE))
        pl.semaphore_signal(barrier, inc=1, device_id=other, device_id_type=MESH)
    for step in (1, -1, SLOTS - 1, 1 - SLOTS, SLOTS, -SLOTS):
        pl.semaphore_signal(barrier, inc=1, device_id=along(step), device_id_type=MESH)
    pl.semaphore_wait(barrier, GROUP_SIZE + 5)

    my_rows = pl.ds(pl.multiple_of(own_row + me * rows, rows), rows)
    for half in range(2):
        for which, src in enumerate((k_ref, v_ref)):
            dst = windows[which][half]
            for k in range(GROUP_SIZE):
                index = lax.rem(me + k, GROUP_SIZE)
                cols = pl.ds(pl.multiple_of(index * HD, HD), HD)
                if k:
                    pltpu.make_async_remote_copy(
                        src.at[half, :, cols],
                        dst.at[my_rows, :],
                        sent.at[which],
                        own_sem.at[which, half],
                        device_id=member(index),
                        device_id_type=MESH,
                    ).start()
                else:
                    pltpu.make_async_copy(
                        src.at[half, :, cols], dst.at[my_rows, :], own_sem.at[which, half]
                    ).start()

    q_rows = pl.ds(pl.multiple_of(me * rows, rows), rows)
    for half in range(2):
        for k in range(GROUP_SIZE):
            index = lax.rem(me + k, GROUP_SIZE)
            cols = pl.ds(pl.multiple_of(index * wide, wide), wide)
            if k:
                pltpu.make_async_remote_copy(
                    q_ref.at[half, :, cols],
                    q_all.at[half, q_rows, :],
                    sent.at[2],
                    q_sem.at[half],
                    device_id=member(index),
                    device_id_type=MESH,
                ).start()
            else:
                pltpu.make_async_copy(q_ref.at[half, :, cols], q_all.at[half, q_rows, :], q_sem.at[half]).start()

    def slot_rows(slot):
        return pl.ds((SLOTS - 1 - slot) * span, span)

    def hop(which, half, source, to_slot, step, sem, left):
        crossed = (group + step + groups) // groups - 1

        def to(to_half):
            pltpu.make_async_remote_copy(
                source,
                windows[which][to_half].at[slot_rows(to_slot), :],
                left.at[which, half],
                sem.at[to_half],
                device_id=along(step),
                device_id_type=MESH,
            ).start()

        pl.when(crossed == 0)(lambda: to(half))
        pl.when(crossed != 0)(lambda: to(1 - half))

    def arrived(which, half, slot, sem):
        ref = windows[which][half].at[slot_rows(slot), :]
        pltpu.make_async_copy(ref, ref, sem.at[half]).wait()

    for half in range(2):
        for part in range(2):
            first = half * half_len + group * span + part * block
            pos = first + lax.broadcasted_iota(jnp.int32, (block, 1), 0)

            def one_doc(i, carry):
                end, begin = carry
                end = end + len_ref[i]
                return end, jnp.where(pos >= end, end, begin)

            _, begin = lax.fori_loop(0, len_ref.shape[0], one_doc, (jnp.int32(0), jnp.zeros((block, 1), jnp.int32)))
            key_pos = first - (window - block) + lax.broadcasted_iota(jnp.int32, (1, window), 1)
            allowed = (key_pos >= begin) & (key_pos <= pos)
            bias[half * 2 + part] = jnp.where(allowed, 0.0, NEG_FILL)

    awaited = set()

    def pass_on(way, slot, half, which):
        source = windows[which][half].at[slot_rows(slot), :]
        if slot == 0 and (half, which) not in awaited:
            awaited.add((half, which))
            arrived(which, half, 0, own_sem.at[which])
        if way == "up":
            if slot > 0:
                arrived(which, half, slot, up_sem.at[slot - 1, which])
            if slot < 3 or (slot == 3 and which == 0):
                hop(which, half, source, slot + 1, 1, up_sem.at[slot, which], chain_sent)
        elif way == "relay":

            @pl.when(place == RING - 2)
            def _():
                ref = relayed.at[which, half]
                pltpu.make_async_copy(ref, ref, relay_sem.at[which, half]).wait()
                hop(which, half, ref, SLOTS - 1, SLOTS, down_sem.at[0, which], relay_sent)

        elif slot == 0:

            @pl.when(place != RING - 1)
            def _():
                hop(which, half, source, SLOTS - 1, SLOTS - 1, down_sem.at[0, which], chain_sent)

            @pl.when(place == RING - 1)
            def _():
                pltpu.make_async_remote_copy(
                    source,
                    relayed.at[which, half],
                    chain_sent.at[which, half],
                    relay_sem.at[which, half],
                    device_id=along(-1),
                    device_id_type=MESH,
                ).start()

        else:
            arrived(which, half, slot, down_sem.at[6 - slot, which])
            if slot == 6 or (slot == 5 and which == 1):
                hop(which, half, source, slot - 1, -1, down_sem.at[7 - slot, which], chain_sent)

    def unit(u, half):
        part = u // 2
        side = lax.rem(u, 2)
        row0 = pl.multiple_of(part * block, block)
        col0 = pl.multiple_of(side * (wide // 2), wide // 2)
        keys_from = pl.multiple_of(block + part * block, block)
        queries = jnp.concatenate(
            [
                q_all[half, pl.ds(row0, block), pl.ds(pl.multiple_of(col0 + i * HD, HD), HD)]
                for i in range(GROUP // 2)
            ],
            axis=0,
        )
        keys = windows[0][half][pl.ds(keys_from, window), :]
        for tile in range(window // 256):
            part_keys = keys[tile * 256 : (tile + 1) * 256]
            product = lax.dot_general(
                queries, part_keys, (((1,), (1,)), ((), ())), preferred_element_type=jnp.float32
            )
            add = bias[half * 2 + part, :, tile * 256 : (tile + 1) * 256]
            scores[:, tile * 256 : (tile + 1) * 256] = (
                product.reshape(GROUP // 2, block, 256) + add[None]
            ).reshape(GROUP // 2 * block, 256)
        values = windows[1][half][pl.ds(keys_from, window), :]
        values = jnp.concatenate([values, jnp.ones_like(values)], axis=1)
        for i in range(GROUP // 2):
            s = scores[i * block : (i + 1) * block, :]
            top = jnp.max(s, axis=1, keepdims=True)
            weight = jnp.exp2((s - top) * FACTOR).astype(jnp.bfloat16)
            mixed = jnp.dot(weight, values, preferred_element_type=jnp.float32)
            o_all[half * 4 + u, :, i * HD : (i + 1) * HD] = (mixed[:, :HD] / mixed[:, HD:]).astype(jnp.bfloat16)
        for k in range(SIDE):
            to_x = lax.rem(x + k, SIDE)
            src = o_all.at[half * 4 + u, pl.ds(pl.multiple_of(to_x * rows, rows), rows), :]
            dst = out_ref.at[half, :, pl.ds(pl.multiple_of(me * wide + col0, wide // 2), wide // 2)]

            def remote():
                pltpu.make_async_remote_copy(
                    src,
                    dst,
                    sent.at[3],
                    out_sem,
                    device_id=(group * 2 + part, to_x),
                    device_id_type=MESH,
                ).start()

            if k:
                remote()
            else:
                pl.when(part != core)(remote)

                @pl.when(part == core)
                def _():
                    pltpu.make_async_copy(src, dst, out_sem).start()

        return 0

    for entry in ORDER:
        if entry:
            pass_on(*entry)
        else:
            for half in range(2):
                pltpu.make_async_copy(q_all.at[half], q_all.at[half], q_sem.at[half]).wait()
            lax.fori_loop(0, 4, lambda u, _: unit(u, 0), 0)
    lax.fori_loop(0, 4, lambda u, _: unit(u, 1), 0)

    pltpu.make_async_copy(out_ref, out_ref, out_sem).wait()
    others = k_ref.at[:, :, : (GROUP_SIZE - 1) * HD]
    pltpu.make_async_copy(others, others, sent.at[0]).wait()
    pltpu.make_async_copy(others, others, sent.at[1]).wait()
    others = q_ref.at[:, :, : (GROUP_SIZE - 1) * wide]
    pltpu.make_async_copy(others, others, sent.at[2]).wait()
    pltpu.make_async_copy(others, others, sent.at[3]).wait()
    for which in range(2):
        for half in range(2):
            hops = windows[which][half].at[pl.ds(0, 6 * span), :]
            pltpu.make_async_copy(hops, hops, chain_sent.at[which, half]).wait()

            @pl.when(place == RING - 2)
            def _(which=which, half=half):
                ref = relayed.at[which, half]
                pltpu.make_async_copy(ref, ref, relay_sent.at[which, half]).wait()


def per_device(queries, keys, values, doc_lengths):
    rows = queries.shape[1]
    groups = lax.axis_size("ctx") // 2
    half_len = rows * GROUP_SIZE * groups
    span = rows * GROUP_SIZE
    block = span // 2
    window = (SLOTS - 1) * span
    pairs = 2 * span * GROUP
    body = functools.partial(attention_kernel, rows, groups, half_len)
    anywhere = pl.BlockSpec(memory_space=pl.ANY)
    return pl.pallas_call(
        body,
        out_shape=jax.ShapeDtypeStruct(queries.shape, queries.dtype),
        in_specs=[anywhere, anywhere, anywhere, pl.BlockSpec(memory_space=pltpu.SMEM)],
        out_specs=anywhere,
        scratch_shapes=[
            pltpu.VMEM((2, span, GROUP * HD), jnp.bfloat16),
            pltpu.VMEM((SLOTS * span, HD), jnp.bfloat16),
            pltpu.VMEM((SLOTS * span, HD), jnp.bfloat16),
            pltpu.VMEM((SLOTS * span, HD), jnp.bfloat16),
            pltpu.VMEM((SLOTS * span, HD), jnp.bfloat16),
            pltpu.VMEM((2, 2, span, HD), jnp.bfloat16),
            pltpu.VMEM((8, block, GROUP // 2 * HD), jnp.bfloat16),
            pltpu.VMEM((4, block, window), jnp.float32),
            pltpu.VMEM((GROUP // 2 * block, window), jnp.float32),
            pltpu.SemaphoreType.DMA((4,)),
            pltpu.SemaphoreType.DMA((2, 2)),
            pltpu.SemaphoreType.DMA((2,)),
            pltpu.SemaphoreType.DMA((4, 2, 2)),
            pltpu.SemaphoreType.DMA((3, 2, 2)),
            pltpu.SemaphoreType.DMA((2, 2)),
            pltpu.SemaphoreType.DMA((2, 2)),
            pltpu.SemaphoreType.DMA((2, 2)),
            pltpu.SemaphoreType.DMA,
        ],
        compiler_params=pltpu.CompilerParams(
            collective_id=0, has_side_effects=True, vmem_limit_bytes=63 << 20
        ),
        cost_estimate=pl.CostEstimate(
            flops=4 * pairs * window * HD, bytes_accessed=5 << 20, transcendentals=pairs * window
        ),
    )(queries, keys, values, doc_lengths)


def solution(mesh):
    placed = P(None, ("ctx", "head"), None)
    return jax.shard_map(
        per_device,
        mesh=mesh,
        in_specs=(placed, placed, placed, P()),
        out_specs=placed,
        check_vma=False,
    )
```

```python
import functools
import math

import jax
import jax.numpy as jnp
from jax import lax
from jax.experimental import pallas as pl
from jax.experimental.pallas import tpu as pltpu
from jax.sharding import PartitionSpec as P

MESH = pl.DeviceIdType.MESH
HD = 128
HEADS = 8
GROUP = 8
SIDE = 4
GROUP_SIZE = 8
SLOTS = 7
OWN = 8
RING = 8
NEG_FILL = -1e30
ORDER = (
    ("up", 0, 0, 0), ("up", 0, 1, 0), ("down", 0, 0, 0), ("down", 0, 1, 0),
    ("up", 0, 0, 1), ("up", 0, 1, 1), ("down", 0, 0, 1), ("down", 0, 1, 1),
    ("up", 1, 0, 0), ("up", 1, 1, 0), ("up", 1, 0, 1), ("up", 1, 1, 1),
    ("up", 2, 0, 0), ("up", 2, 1, 0), ("up", 2, 0, 1), ("up", 2, 1, 1),
    ("relay", 0, 0, 0), ("relay", 0, 1, 0), ("relay", 0, 0, 1), ("relay", 0, 1, 1),
    ("down", 6, 0, 0), ("down", 6, 1, 0), ("down", 6, 0, 1), ("down", 6, 1, 1),
    ("up", 3, 0, 0), ("up", 3, 1, 0), ("up", 3, 0, 1), ("up", 3, 1, 1),
    ("down", 5, 0, 0), ("down", 5, 1, 0), ("down", 5, 0, 1), ("down", 5, 1, 1),
    ("up", 4, 0, 0), ("down", 4, 0, 1), (), ("up", 4, 1, 0), ("down", 4, 1, 1),
)
FACTOR = 1.0 / math.sqrt(HD) * math.log2(math.e)


def attention_kernel(
    rows,
    groups,
    half_len,
    q_ref,
    k_ref,
    v_ref,
    len_ref,
    out_ref,
    q_all,
    k_low,
    k_high,
    v_low,
    v_high,
    relayed,
    o_all,
    bias,
    scores,
    sent,
    own_sem,
    q_sem,
    up_sem,
    down_sem,
    chain_sent,
    relay_sem,
    relay_sent,
    out_sem,
):
    ctx = lax.axis_index("ctx")
    x = lax.axis_index("head")
    core = lax.rem(ctx, 2)
    group = ctx // 2
    place = lax.rem(group, RING)
    me = core * SIDE + x
    span = rows * GROUP_SIZE
    block = span // 2
    wide = GROUP * HD
    own_row = (SLOTS - 1) * span
    window = (SLOTS - 2) * span + 2 * block

    windows = ((k_low, k_high), (v_low, v_high))

    def member(index):
        return (group * 2 + index // SIDE, lax.rem(index, SIDE))

    def along(step):
        return (lax.rem(group + step + groups, groups) * 2 + core, x)

    barrier = pltpu.get_barrier_semaphore()
    for k in range(1, GROUP_SIZE):
        other = member(lax.rem(me + k, GROUP_SIZE))
        pl.semaphore_signal(barrier, inc=1, device_id=other, device_id_type=MESH)
    for step in (1, -1, SLOTS - 1, 1 - SLOTS, SLOTS, -SLOTS):
        pl.semaphore_signal(barrier, inc=1, device_id=along(step), device_id_type=MESH)
    pl.semaphore_wait(barrier, GROUP_SIZE + 5)

    my_rows = pl.ds(pl.multiple_of(own_row + me * rows, rows), rows)
    for which, src in enumerate((k_ref, v_ref)):
        for half in range(2):
            dst = windows[which][half]
            for k in range(GROUP_SIZE):
                index = lax.rem(me + k, GROUP_SIZE)
                cols = pl.ds(pl.multiple_of(index * HD, HD), HD)
                if k:
                    pltpu.make_async_remote_copy(
                        src.at[half, :, cols],
                        dst.at[my_rows, :],
                        sent.at[which],
                        own_sem.at[which, half],
                        device_id=member(index),
                        device_id_type=MESH,
                    ).start()
                else:
                    pltpu.make_async_copy(
                        src.at[half, :, cols], dst.at[my_rows, :], own_sem.at[which, half]
                    ).start()

    def slot_rows(slot):
        return pl.ds((SLOTS - 1 - slot) * span, span)

    def hop(which, half, source, to_slot, step, sem, left):
        crossed = (group + step + groups) // groups - 1

        def to(to_half):
            pltpu.make_async_remote_copy(
                source,
                windows[which][to_half].at[slot_rows(to_slot), :],
                left.at[which, half],
                sem.at[to_half],
                device_id=along(step),
                device_id_type=MESH,
            ).start()

        pl.when(crossed == 0)(lambda: to(half))
        pl.when(crossed != 0)(lambda: to(1 - half))

    def arrived(which, half, slot, sem):
        ref = windows[which][half].at[slot_rows(slot), :]
        pltpu.make_async_copy(ref, ref, sem.at[half]).wait()

    awaited = set()

    def pass_on(way, slot, half, which):
        source = windows[which][half].at[slot_rows(slot), :]
        if slot == 0 and (half, which) not in awaited:
            awaited.add((half, which))
            arrived(which, half, 0, own_sem.at[which])
        if way == "up":
            if slot > 0:
                arrived(which, half, slot, up_sem.at[slot - 1, which])
            if slot < 3 or (slot == 3 and which == 0):
                hop(which, half, source, slot + 1, 1, up_sem.at[slot, which], chain_sent)
        elif way == "relay":

            @pl.when(place == RING - 2)
            def _():
                ref = relayed.at[which, half]
                pltpu.make_async_copy(ref, ref, relay_sem.at[which, half]).wait()
                hop(which, half, ref, SLOTS - 1, SLOTS, down_sem.at[0, which], relay_sent)

        elif slot == 0:

            @pl.when(place != RING - 1)
            def _():
                hop(which, half, source, SLOTS - 1, SLOTS - 1, down_sem.at[0, which], chain_sent)

            @pl.when(place == RING - 1)
            def _():
                pltpu.make_async_remote_copy(
                    source,
                    relayed.at[which, half],
                    chain_sent.at[which, half],
                    relay_sem.at[which, half],
                    device_id=along(-1),
                    device_id_type=MESH,
                ).start()

        else:
            arrived(which, half, slot, down_sem.at[6 - slot, which])
            if slot == 6 or (slot == 5 and which == 1):
                hop(which, half, source, slot - 1, -1, down_sem.at[7 - slot, which], chain_sent)

    for entry in ORDER[:OWN]:
        pass_on(*entry)

    q_rows = pl.ds(pl.multiple_of(me * rows, rows), rows)
    for half in range(2):
        for k in range(GROUP_SIZE):
            index = lax.rem(me + k, GROUP_SIZE)
            cols = pl.ds(pl.multiple_of(index * wide, wide), wide)
            if k:
                pltpu.make_async_remote_copy(
                    q_ref.at[half, :, cols],
                    q_all.at[half, q_rows, :],
                    sent.at[2],
                    q_sem.at[half],
                    device_id=member(index),
                    device_id_type=MESH,
                ).start()
            else:
                pltpu.make_async_copy(q_ref.at[half, :, cols], q_all.at[half, q_rows, :], q_sem.at[half]).start()

    for half in range(2):
        for part in range(2):
            first = half * half_len + group * span + part * block
            pos = first + lax.broadcasted_iota(jnp.int32, (block, 1), 0)

            def one_doc(i, carry):
                end, begin = carry
                end = end + len_ref[i]
                return end, jnp.where(pos >= end, end, begin)

            _, begin = lax.fori_loop(0, len_ref.shape[0], one_doc, (jnp.int32(0), jnp.zeros((block, 1), jnp.int32)))
            key_pos = first - (window - block) + lax.broadcasted_iota(jnp.int32, (1, window), 1)
            allowed = (key_pos >= begin) & (key_pos <= pos)
            bias[half * 2 + part] = jnp.where(allowed, 0.0, NEG_FILL)

    def unit(u, half):
        part = u // 2
        side = lax.rem(u, 2)
        row0 = pl.multiple_of(part * block, block)
        col0 = pl.multiple_of(side * (wide // 2), wide // 2)
        keys_from = pl.multiple_of(block + part * block, block)
        queries = jnp.concatenate(
            [
                q_all[half, pl.ds(row0, block), pl.ds(pl.multiple_of(col0 + i * HD, HD), HD)]
                for i in range(GROUP // 2)
            ],
            axis=0,
        )
        keys = windows[0][half][pl.ds(keys_from, window), :]
        for tile in range(window // 256):
            part_keys = keys[tile * 256 : (tile + 1) * 256]
            product = lax.dot_general(
                queries, part_keys, (((1,), (1,)), ((), ())), preferred_element_type=jnp.float32
            )
            add = bias[half * 2 + part, :, tile * 256 : (tile + 1) * 256]
            scores[:, tile * 256 : (tile + 1) * 256] = (
                product.reshape(GROUP // 2, block, 256) + add[None]
            ).reshape(GROUP // 2 * block, 256)
        values = windows[1][half][pl.ds(keys_from, window), :]
        values = jnp.concatenate([values, jnp.ones_like(values)], axis=1)
        for i in range(GROUP // 2):
            s = scores[i * block : (i + 1) * block, :]
            top = jnp.max(s, axis=1, keepdims=True)
            weight = jnp.exp2((s - top) * FACTOR).astype(jnp.bfloat16)
            mixed = jnp.dot(weight, values, preferred_element_type=jnp.float32)
            o_all[half * 4 + u, :, i * HD : (i + 1) * HD] = (mixed[:, :HD] / mixed[:, HD:]).astype(jnp.bfloat16)
        for k in range(SIDE):
            to_x = lax.rem(x + k, SIDE)
            src = o_all.at[half * 4 + u, pl.ds(pl.multiple_of(to_x * rows, rows), rows), :]
            dst = out_ref.at[half, :, pl.ds(pl.multiple_of(me * wide + col0, wide // 2), wide // 2)]

            def remote():
                pltpu.make_async_remote_copy(
                    src,
                    dst,
                    sent.at[3],
                    out_sem,
                    device_id=(group * 2 + part, to_x),
                    device_id_type=MESH,
                ).start()

            if k:
                remote()
            else:
                pl.when(part != core)(remote)

                @pl.when(part == core)
                def _():
                    pltpu.make_async_copy(src, dst, out_sem).start()

        return 0

    for entry in ORDER[OWN:]:
        if entry:
            pass_on(*entry)
        else:
            for half in range(2):
                pltpu.make_async_copy(q_all.at[half], q_all.at[half], q_sem.at[half]).wait()
            lax.fori_loop(0, 4, lambda u, _: unit(u, 0), 0)
    lax.fori_loop(0, 4, lambda u, _: unit(u, 1), 0)

    pltpu.make_async_copy(out_ref, out_ref, out_sem).wait()
    others = k_ref.at[:, :, : (GROUP_SIZE - 1) * HD]
    pltpu.make_async_copy(others, others, sent.at[0]).wait()
    pltpu.make_async_copy(others, others, sent.at[1]).wait()
    others = q_ref.at[:, :, : (GROUP_SIZE - 1) * wide]
    pltpu.make_async_copy(others, others, sent.at[2]).wait()
    pltpu.make_async_copy(others, others, sent.at[3]).wait()
    for which in range(2):
        for half in range(2):
            hops = windows[which][half].at[pl.ds(0, 6 * span), :]
            pltpu.make_async_copy(hops, hops, chain_sent.at[which, half]).wait()

            @pl.when(place == RING - 2)
            def _(which=which, half=half):
                ref = relayed.at[which, half]
                pltpu.make_async_copy(ref, ref, relay_sent.at[which, half]).wait()


def per_device(queries, keys, values, doc_lengths):
    rows = queries.shape[1]
    groups = lax.axis_size("ctx") // 2
    half_len = rows * GROUP_SIZE * groups
    span = rows * GROUP_SIZE
    block = span // 2
    window = (SLOTS - 1) * span
    pairs = 2 * span * GROUP
    body = functools.partial(attention_kernel, rows, groups, half_len)
    anywhere = pl.BlockSpec(memory_space=pl.ANY)
    return pl.pallas_call(
        body,
        out_shape=jax.ShapeDtypeStruct(queries.shape, queries.dtype),
        in_specs=[anywhere, anywhere, anywhere, pl.BlockSpec(memory_space=pltpu.SMEM)],
        out_specs=anywhere,
        scratch_shapes=[
            pltpu.VMEM((2, span, GROUP * HD), jnp.bfloat16),
            pltpu.VMEM((SLOTS * span, HD), jnp.bfloat16),
            pltpu.VMEM((SLOTS * span, HD), jnp.bfloat16),
            pltpu.VMEM((SLOTS * span, HD), jnp.bfloat16),
            pltpu.VMEM((SLOTS * span, HD), jnp.bfloat16),
            pltpu.VMEM((2, 2, span, HD), jnp.bfloat16),
            pltpu.VMEM((8, block, GROUP // 2 * HD), jnp.bfloat16),
            pltpu.VMEM((4, block, window), jnp.float32),
            pltpu.VMEM((GROUP // 2 * block, window), jnp.float32),
            pltpu.SemaphoreType.DMA((4,)),
            pltpu.SemaphoreType.DMA((2, 2)),
            pltpu.SemaphoreType.DMA((2,)),
            pltpu.SemaphoreType.DMA((4, 2, 2)),
            pltpu.SemaphoreType.DMA((3, 2, 2)),
            pltpu.SemaphoreType.DMA((2, 2)),
            pltpu.SemaphoreType.DMA((2, 2)),
            pltpu.SemaphoreType.DMA((2, 2)),
            pltpu.SemaphoreType.DMA,
        ],
        compiler_params=pltpu.CompilerParams(
            collective_id=0, has_side_effects=True, vmem_limit_bytes=63 << 20
        ),
        cost_estimate=pl.CostEstimate(
            flops=4 * pairs * window * HD, bytes_accessed=5 << 20, transcendentals=pairs * window
        ),
    )(queries, keys, values, doc_lengths)


def solution(mesh):
    placed = P(None, ("ctx", "head"), None)
    return jax.shard_map(
        per_device,
        mesh=mesh,
        in_specs=(placed, placed, placed, P()),
        out_specs=placed,
        check_vma=False,
    )
```

```python
import functools
import math

import jax
import jax.numpy as jnp
from jax import lax
from jax.experimental import pallas as pl
from jax.experimental.pallas import tpu as pltpu
from jax.sharding import PartitionSpec as P

MESH = pl.DeviceIdType.MESH
HD = 128
HEADS = 8
GROUP = 8
SIDE = 4
GROUP_SIZE = 8
SLOTS = 7
OWN = 8
RING = 8
NEG_FILL = -1e30
ORDER = (
    ("up", 0, 0, 0), ("up", 0, 1, 0), ("down", 0, 0, 0), ("down", 0, 1, 0),
    ("up", 0, 0, 1), ("up", 0, 1, 1), ("down", 0, 0, 1), ("down", 0, 1, 1),
    ("up", 1, 0, 0), ("up", 1, 1, 0), ("up", 1, 0, 1), ("up", 1, 1, 1),
    ("up", 2, 0, 0), ("up", 2, 1, 0), ("up", 2, 0, 1), ("up", 2, 1, 1),
    ("relay", 0, 0, 0), ("relay", 0, 1, 0), ("relay", 0, 0, 1), ("relay", 0, 1, 1),
    ("down", 6, 0, 0), ("down", 6, 1, 0), ("down", 6, 0, 1), ("down", 6, 1, 1),
    ("up", 3, 0, 0), ("up", 3, 1, 0), ("up", 3, 0, 1), ("up", 3, 1, 1),
    ("down", 5, 0, 0), ("down", 5, 1, 0), ("down", 5, 0, 1), ("down", 5, 1, 1),
    ("up", 4, 0, 0), ("down", 4, 0, 1), (), ("up", 4, 1, 0), ("down", 4, 1, 1),
)
FACTOR = 1.0 / math.sqrt(HD) * math.log2(math.e)


def attention_kernel(
    rows,
    groups,
    half_len,
    q_ref,
    k_ref,
    v_ref,
    len_ref,
    out_ref,
    q_all,
    k_low,
    k_high,
    v_low,
    v_high,
    relayed,
    o_all,
    bias,
    scores,
    sent,
    own_sem,
    q_sem,
    up_sem,
    down_sem,
    chain_sent,
    relay_sem,
    relay_sent,
    out_sem,
):
    ctx = lax.axis_index("ctx")
    x = lax.axis_index("head")
    core = lax.rem(ctx, 2)
    group = ctx // 2
    place = lax.rem(group, RING)
    me = core * SIDE + x
    span = rows * GROUP_SIZE
    block = span // 2
    wide = GROUP * HD
    own_row = (SLOTS - 1) * span
    window = (SLOTS - 2) * span + 2 * block

    windows = ((k_low, k_high), (v_low, v_high))

    def member(index):
        return (group * 2 + index // SIDE, lax.rem(index, SIDE))

    def along(step):
        return (lax.rem(group + step + groups, groups) * 2 + core, x)

    barrier = pltpu.get_barrier_semaphore()
    for k in range(1, GROUP_SIZE):
        other = member(lax.rem(me + k, GROUP_SIZE))
        pl.semaphore_signal(barrier, inc=1, device_id=other, device_id_type=MESH)
    for step in (1, -1, SLOTS - 1, 1 - SLOTS, SLOTS, -SLOTS):
        pl.semaphore_signal(barrier, inc=1, device_id=along(step), device_id_type=MESH)
    pl.semaphore_wait(barrier, GROUP_SIZE + 5)

    my_rows = pl.ds(pl.multiple_of(own_row + me * rows, rows), rows)
    for which, src in enumerate((k_ref, v_ref)):
        for half in range(2):
            dst = windows[which][half]
            for k in range(GROUP_SIZE):
                index = lax.rem(me + k, GROUP_SIZE)
                cols = pl.ds(pl.multiple_of(index * HD, HD), HD)
                if k:
                    pltpu.make_async_remote_copy(
                        src.at[half, :, cols],
                        dst.at[my_rows, :],
                        sent.at[which],
                        own_sem.at[which, half],
                        device_id=member(index),
                        device_id_type=MESH,
                    ).start()
                else:
                    pltpu.make_async_copy(
                        src.at[half, :, cols], dst.at[my_rows, :], own_sem.at[which, half]
                    ).start()

    def slot_rows(slot):
        return pl.ds((SLOTS - 1 - slot) * span, span)

    def hop(which, half, source, to_slot, step, sem, left):
        crossed = (group + step + groups) // groups - 1

        def to(to_half):
            pltpu.make_async_remote_copy(
                source,
                windows[which][to_half].at[slot_rows(to_slot), :],
                left.at[which, half],
                sem.at[to_half],
                device_id=along(step),
                device_id_type=MESH,
            ).start()

        pl.when(crossed == 0)(lambda: to(half))
        pl.when(crossed != 0)(lambda: to(1 - half))

    def arrived(which, half, slot, sem):
        ref = windows[which][half].at[slot_rows(slot), :]
        pltpu.make_async_copy(ref, ref, sem.at[half]).wait()

    awaited = set()

    def pass_on(way, slot, half, which):
        source = windows[which][half].at[slot_rows(slot), :]
        if slot == 0 and (half, which) not in awaited:
            awaited.add((half, which))
            arrived(which, half, 0, own_sem.at[which])
        if way == "up":
            if slot > 0:
                arrived(which, half, slot, up_sem.at[slot - 1, which])
            if slot < 3 or (slot == 3 and which == 0):
                hop(which, half, source, slot + 1, 1, up_sem.at[slot, which], chain_sent)
        elif way == "relay":

            @pl.when(place == RING - 2)
            def _():
                ref = relayed.at[which, half]
                pltpu.make_async_copy(ref, ref, relay_sem.at[which, half]).wait()
                hop(which, half, ref, SLOTS - 1, SLOTS, down_sem.at[0, which], relay_sent)

        elif slot == 0:

            @pl.when(place != RING - 1)
            def _():
                hop(which, half, source, SLOTS - 1, SLOTS - 1, down_sem.at[0, which], chain_sent)

            @pl.when(place == RING - 1)
            def _():
                pltpu.make_async_remote_copy(
                    source,
                    relayed.at[which, half],
                    chain_sent.at[which, half],
                    relay_sem.at[which, half],
                    device_id=along(-1),
                    device_id_type=MESH,
                ).start()

        else:
            arrived(which, half, slot, down_sem.at[6 - slot, which])
            if slot == 6 or (slot == 5 and which == 1):
                hop(which, half, source, slot - 1, -1, down_sem.at[7 - slot, which], chain_sent)

    for entry in ORDER[:OWN]:
        pass_on(*entry)

    q_rows = pl.ds(pl.multiple_of(me * rows, rows), rows)
    for half in range(2):
        for k in range(GROUP_SIZE):
            index = lax.rem(me + k, GROUP_SIZE)
            cols = pl.ds(pl.multiple_of(index * wide, wide), wide)
            if k:
                pltpu.make_async_remote_copy(
                    q_ref.at[half, :, cols],
                    q_all.at[half, q_rows, :],
                    sent.at[2],
                    q_sem.at[half],
                    device_id=member(index),
                    device_id_type=MESH,
                ).start()
            else:
                pltpu.make_async_copy(q_ref.at[half, :, cols], q_all.at[half, q_rows, :], q_sem.at[half]).start()

    for half in range(2):
        for part in range(2):
            first = half * half_len + group * span + part * block
            pos = first + lax.broadcasted_iota(jnp.int32, (block, 1), 0)

            def one_doc(i, carry):
                end, begin = carry
                end = end + len_ref[i]
                return end, jnp.where(pos >= end, end, begin)

            _, begin = lax.fori_loop(0, len_ref.shape[0], one_doc, (jnp.int32(0), jnp.zeros((block, 1), jnp.int32)))
            key_pos = first - (window - block) + lax.broadcasted_iota(jnp.int32, (1, window), 1)
            allowed = (key_pos >= begin) & (key_pos <= pos)
            bias[half * 2 + part] = jnp.where(allowed, 0.0, NEG_FILL)

    def unit(u, half):
        part = u // 2
        side = lax.rem(u, 2)
        row0 = pl.multiple_of(part * block, block)
        col0 = pl.multiple_of(side * (wide // 2), wide // 2)
        keys_from = pl.multiple_of(block + part * block, block)
        queries = jnp.concatenate(
            [
                q_all[half, pl.ds(row0, block), pl.ds(pl.multiple_of(col0 + i * HD, HD), HD)]
                for i in range(GROUP // 2)
            ],
            axis=0,
        )
        keys = windows[0][half][pl.ds(keys_from, window), :]
        for tile in range(window // 256):
            part_keys = keys[tile * 256 : (tile + 1) * 256]
            product = lax.dot_general(
                queries, part_keys, (((1,), (1,)), ((), ())), preferred_element_type=jnp.float32
            )
            add = bias[half * 2 + part, :, tile * 256 : (tile + 1) * 256]
            scores[:, tile * 256 : (tile + 1) * 256] = (
                product.reshape(GROUP // 2, block, 256) + add[None]
            ).reshape(GROUP // 2 * block, 256)
        values = windows[1][half][pl.ds(keys_from, window), :]
        values = jnp.concatenate([values, jnp.ones_like(values)], axis=1)
        for i in range(GROUP // 2):
            s = scores[i * block : (i + 1) * block, :]
            top = jnp.max(s, axis=1, keepdims=True)
            weight = jnp.exp2((s - top) * FACTOR).astype(jnp.bfloat16)
            mixed = jnp.dot(weight, values, preferred_element_type=jnp.float32)
            o_all[half * 4 + u, :, i * HD : (i + 1) * HD] = (mixed[:, :HD] / mixed[:, HD:]).astype(jnp.bfloat16)
        for k in (2, 1, 3, 0):
            to_x = lax.rem(x + k, SIDE)
            src = o_all.at[half * 4 + u, pl.ds(pl.multiple_of(to_x * rows, rows), rows), :]
            dst = out_ref.at[half, :, pl.ds(pl.multiple_of(me * wide + col0, wide // 2), wide // 2)]

            def remote():
                pltpu.make_async_remote_copy(
                    src,
                    dst,
                    sent.at[3],
                    out_sem,
                    device_id=(group * 2 + part, to_x),
                    device_id_type=MESH,
                ).start()

            if k:
                remote()
            else:
                pl.when(part != core)(remote)

                @pl.when(part == core)
                def _():
                    pltpu.make_async_copy(src, dst, out_sem).start()

        return 0

    for entry in ORDER[OWN:]:
        if entry:
            pass_on(*entry)
        else:
            for half in range(2):
                pltpu.make_async_copy(q_all.at[half], q_all.at[half], q_sem.at[half]).wait()
            lax.fori_loop(0, 4, lambda u, _: unit(u, 0), 0)
    lax.fori_loop(0, 4, lambda u, _: unit(u, 1), 0)

    pltpu.make_async_copy(out_ref, out_ref, out_sem).wait()
    others = k_ref.at[:, :, : (GROUP_SIZE - 1) * HD]
    pltpu.make_async_copy(others, others, sent.at[0]).wait()
    pltpu.make_async_copy(others, others, sent.at[1]).wait()
    others = q_ref.at[:, :, : (GROUP_SIZE - 1) * wide]
    pltpu.make_async_copy(others, others, sent.at[2]).wait()
    pltpu.make_async_copy(others, others, sent.at[3]).wait()
    for which in range(2):
        for half in range(2):
            hops = windows[which][half].at[pl.ds(0, 6 * span), :]
            pltpu.make_async_copy(hops, hops, chain_sent.at[which, half]).wait()

            @pl.when(place == RING - 2)
            def _(which=which, half=half):
                ref = relayed.at[which, half]
                pltpu.make_async_copy(ref, ref, relay_sent.at[which, half]).wait()


def per_device(queries, keys, values, doc_lengths):
    rows = queries.shape[1]
    groups = lax.axis_size("ctx") // 2
    half_len = rows * GROUP_SIZE * groups
    span = rows * GROUP_SIZE
    block = span // 2
    window = (SLOTS - 1) * span
    pairs = 2 * span * GROUP
    body = functools.partial(attention_kernel, rows, groups, half_len)
    anywhere = pl.BlockSpec(memory_space=pl.ANY)
    return pl.pallas_call(
        body,
        out_shape=jax.ShapeDtypeStruct(queries.shape, queries.dtype),
        in_specs=[anywhere, anywhere, anywhere, pl.BlockSpec(memory_space=pltpu.SMEM)],
        out_specs=anywhere,
        scratch_shapes=[
            pltpu.VMEM((2, span, GROUP * HD), jnp.bfloat16),
            pltpu.VMEM((SLOTS * span, HD), jnp.bfloat16),
            pltpu.VMEM((SLOTS * span, HD), jnp.bfloat16),
            pltpu.VMEM((SLOTS * span, HD), jnp.bfloat16),
            pltpu.VMEM((SLOTS * span, HD), jnp.bfloat16),
            pltpu.VMEM((2, 2, span, HD), jnp.bfloat16),
            pltpu.VMEM((8, block, GROUP // 2 * HD), jnp.bfloat16),
            pltpu.VMEM((4, block, window), jnp.float32),
            pltpu.VMEM((GROUP // 2 * block, window), jnp.float32),
            pltpu.SemaphoreType.DMA((4,)),
            pltpu.SemaphoreType.DMA((2, 2)),
            pltpu.SemaphoreType.DMA((2,)),
            pltpu.SemaphoreType.DMA((4, 2, 2)),
            pltpu.SemaphoreType.DMA((3, 2, 2)),
            pltpu.SemaphoreType.DMA((2, 2)),
            pltpu.SemaphoreType.DMA((2, 2)),
            pltpu.SemaphoreType.DMA((2, 2)),
            pltpu.SemaphoreType.DMA,
        ],
        compiler_params=pltpu.CompilerParams(
            collective_id=0, has_side_effects=True, vmem_limit_bytes=63 << 20
        ),
        cost_estimate=pl.CostEstimate(
            flops=4 * pairs * window * HD, bytes_accessed=5 << 20, transcendentals=pairs * window
        ),
    )(queries, keys, values, doc_lengths)


def solution(mesh):
    placed = P(None, ("ctx", "head"), None)
    return jax.shard_map(
        per_device,
        mesh=mesh,
        in_specs=(placed, placed, placed, P()),
        out_specs=placed,
        check_vma=False,
    )
```
